32 devices in a mesh: traj: 8 (over z, y), mstate: 4 (over x, core).
Axes of the slice: x: 2, y: 2, z: 4, core: 2. Of those that a mesh axis runs over, the one named last changes fastest.
Arguments:
- bias: float32 [32, 262144], P(None, ('traj', 'mstate')), may hold values from -206 to 206
- labels: int32 [262144], P(('traj', 'mstate')), may hold values from 0 to 4095, as said below
- therm_index: int32 [262144], P(('traj', 'mstate')), may hold values from 0 to 31
- counts: int32 [32, 4096, 4096], P(None, 'traj', 'mstate'), may hold values from 0 to 4, as said below
- free_start: float32 [32, 4096], replicated, may hold values from -6 to 6
- mult_start: float32 [32, 4096], replicated, may hold values from -6 to 6
Outputs:
- free_energy: float32 [32, 4096], P(None, 'mstate')
- log_mult: float32 [32, 4096], P(None, 'mstate')
The draws below stay inside these ranges and needn't reach their ends.
Inputs may be any that keep to these rules, and one draw needn't show every extreme that they name: `labels`: every Markov state is the label of at least one frame. `counts`: most entries are zero.
All inputs are finite; a program needn't handle non-finite values.
Results may differ from the reference program's by a relative error of at most 0.0001.
Values sent between devices are 32-bit elements; how exact they have to be, the bound alone decides.
A program may use at most 128 MiB of HBM per device.

```python
import jax
import jax.numpy as jnp
from jax import lax

K = 32
M = 4096
ITERS = 2
FRAMES = 262144


def forced_frames(key):
    return jax.random.permutation(jax.random.fold_in(key, 7), FRAMES)[:M]


def draw_labels(key, part):
    first_key, second_key = jax.random.split(jax.random.fold_in(key, 11), 2)
    first = jax.random.randint(first_key, (FRAMES,), 0, M)
    second = jax.random.randint(second_key, (FRAMES,), 0, M)
    base = jnp.minimum(first, second).astype(jnp.int32)
    chosen = forced_frames(key)
    filled = base.at[chosen].set(jnp.arange(M, dtype=jnp.int32))
    return filled.astype(jnp.int32)


def draw_bias(key, part):
    first_key = jax.random.fold_in(jax.random.fold_in(key, 23), 0)
    values = jnp.clip(2.0 * jax.random.normal(first_key, (K, FRAMES), jnp.float32), -12.0, 12.0)
    return values.astype(jnp.float32)


def draw_counts(key, part):
    place_key, entry_key = jax.random.split(jax.random.fold_in(key, 37))
    place = jax.random.randint(place_key, (K, M, M), 0, M).astype(jnp.int32)
    packed = jax.random.randint(entry_key, (K, M, M), 0, 16777216).astype(jnp.int32)
    present = place < 2
    exponent = jnp.right_shift(packed, 16) % 3
    mantissa = jnp.bitwise_and(jnp.right_shift(packed, 8), 255)
    low_bits = jnp.left_shift(jnp.ones_like(exponent), exponent) - 1
    entry_value = 1 + jnp.bitwise_and(mantissa, low_bits)
    return jnp.where(present, entry_value, 0).astype(jnp.int32)


def set_ends(values, key, smallest, top_value):
    index_at = [jax.random.randint(jax.random.fold_in(key, axis), (), 0, length) for axis, length in enumerate(values.shape)]
    widest = values.shape.index(max(values.shape))
    neighbour = index_at[:widest] + [(index_at[widest] + 1) % values.shape[widest]] + index_at[widest + 1:]
    return values.at[tuple(index_at)].set(smallest).at[tuple(neighbour)].set(top_value)


def normal_values(own_key, extent, width, bound, kind=jnp.bfloat16):
    result = width * jax.random.normal(own_key, extent, jnp.float32)
    return jnp.clip(result, min=-bound, max=bound).astype(kind)


def setup_inputs(seed: int = 0) -> dict:
    splits = jax.random.split(jax.random.key(seed), 7)
    return {
        "bias": draw_bias(jax.random.fold_in(splits[6], 71), 0),
        "labels": draw_labels(jax.random.fold_in(splits[6], 71), 0),
        "therm_index": set_ends(jax.random.randint(splits[2], (FRAMES,), 0, K), jax.random.fold_in(splits[2], 1), 0, K - 1).astype(jnp.int32),
        "counts": draw_counts(jax.random.fold_in(splits[6], 71), 0),
        "free_start": normal_values(splits[4], (K, M), 1.0, 6.0, jnp.float32),
        "mult_start": normal_values(splits[5], (K, M), 1.0, 6.0, jnp.float32),
    }


def update_mult(counts, free, mult):
    def per_state(args):
        block, fk, vk = args
        weight = jax.nn.sigmoid(vk[None, :] + fk[:, None] - vk[:, None] - fk[None, :])
        return jnp.sum(block.astype(fk.dtype) * weight, axis=0)

    total = lax.map(per_state, (counts, free, mult))
    return jnp.log(0.5 + total)


def reference(bias, labels, therm_index, counts, free_start, mult_start):
    ftype = bias.dtype
    states = jax.nn.one_hot(therm_index, K, dtype=ftype)
    visits = jax.ops.segment_sum(states, labels, num_segments=M).T
    free, mult = free_start, mult_start
    for step in range(ITERS):
        mult = update_mult(counts, free, mult)
        level = jnp.log(jnp.exp(mult) + visits) + free
        scores = jnp.take(level, labels, axis=1) - bias
        top = jnp.max(scores, axis=0)
        logl = top + jnp.log(jnp.sum(jnp.exp(scores - top[None, :]), axis=0))
        term = -bias - logl[None, :]
        shift = jnp.max(term, axis=1)
        weights = jnp.exp(term - shift[:, None])
        total = jax.ops.segment_sum(weights.T, labels, num_segments=M).T
        free = -(shift[:, None] + jnp.log(total))
    return free, mult
```

```python
import functools

import jax
import jax.numpy as jnp
from jax import lax
from jax.experimental import pallas as pl
from jax.experimental.pallas import tpu as pltpu
from jax.sharding import PartitionSpec as P

ITERS = 2
LANES = 128
MESH = pl.DeviceIdType.MESH
VMEM = pl.BlockSpec(memory_space=pltpu.VMEM)
LIMIT = 48 * 1024 * 1024


def mult_kernel(where, counts, rows, cols, out, spread):
    k = pl.program_id(0)
    chunks = rows.shape[0]
    for piece in range(cols.shape[0]):
        line = cols[piece, pl.ds(k, 1), :]
        spread[pl.ds(piece * LANES, LANES), :] = jnp.transpose(
            jnp.broadcast_to(line, (LANES, LANES))
        )
    own = [jnp.broadcast_to(rows[c, pl.ds(k, 1), :], (8, LANES)) for c in range(chunks)]

    def body(step, sums):
        at = pl.ds(pl.multiple_of(step * 8, 8), 8)
        other = spread[at, :]
        made = []
        for c in range(chunks):
            number = counts[0, at, c * LANES : (c + 1) * LANES].astype(jnp.float32)
            made.append(sums[c] + number * (1.0 + jnp.tanh(own[c] - other)))
        return tuple(made)

    zero = jnp.zeros((8, LANES), jnp.float32)
    sums = lax.fori_loop(0, counts.shape[1] // 8, body, (zero,) * chunks, unroll=4)
    for c in range(chunks):
        out[c, pl.ds(k, 1), :] = 0.5 * jnp.sum(sums[c], axis=0, keepdims=True)


def mult_partial(where, counts, half):
    states_k, cols, rows = counts.shape
    r, c = rows // LANES, cols // LANES
    return pl.pallas_call(
        mult_kernel,
        grid_spec=pltpu.PrefetchScalarGridSpec(
            num_scalar_prefetch=1,
            grid=(states_k,),
            in_specs=[
                pl.BlockSpec((1, cols, rows), lambda k, w: (k, 0, 0)),
                pl.BlockSpec((r, states_k, LANES), lambda k, w: (w[1], 0, 0)),
                pl.BlockSpec((c, states_k, LANES), lambda k, w: (w[0], 0, 0)),
            ],
            out_specs=pl.BlockSpec((r, states_k, LANES), lambda k, w: (0, 0, 0)),
            scratch_shapes=[pltpu.VMEM((cols, LANES), jnp.float32)],
        ),
        out_shape=jax.ShapeDtypeStruct((r, states_k, LANES), jnp.float32),
        compiler_params=pltpu.CompilerParams(vmem_limit_bytes=LIMIT),
        name="mult_partial",
    )(where, counts, half, half)


def low_onehot(lab):
    low = jnp.bitwise_and(lab, 255)
    lines = lax.broadcasted_iota(jnp.int32, (256, lab.shape[1]), 0)
    return jnp.where(lines == low, 1.0, 0.0).astype(jnp.bfloat16)


def dot_nt(a, b):
    return lax.dot_general(
        a, b, (((1,), (1,)), ((), ())), preferred_element_type=jnp.float32
    )


def visits_kernel(tile, states_k, labels, therm, out, left, acc):
    highs = out.shape[0] // 2
    acc[...] = jnp.zeros_like(acc)

    @pl.loop(0, labels.shape[1] // tile)
    def _(step):
        at = pl.ds(pl.multiple_of(step * tile, tile), tile)
        lab = labels[:, at]
        high = jnp.right_shift(lab, 8)
        lines = lax.broadcasted_iota(jnp.int32, (states_k, tile), 0)
        member = jnp.where(lines == therm[:, at], 1.0, 0.0)
        for h in range(highs):
            left[pl.ds(h * states_k, states_k), :] = jnp.where(
                high == h, member, 0.0
            ).astype(jnp.bfloat16)
        acc[...] += dot_nt(left[...], low_onehot(lab))

    for h in range(highs):
        at = pl.ds(h * states_k, states_k)
        out[2 * h] = acc[at, :LANES]
        out[2 * h + 1] = acc[at, LANES:]


def local_visits(labels, therm, states_k, width):
    tile = 1024
    rows = width // 256 * states_k
    return pl.pallas_call(
        functools.partial(visits_kernel, tile, states_k),
        out_shape=jax.ShapeDtypeStruct((width // LANES, states_k, LANES), jnp.float32),
        in_specs=[VMEM] * 2,
        out_specs=VMEM,
        scratch_shapes=[
            pltpu.VMEM((rows, tile), jnp.bfloat16),
            pltpu.VMEM((rows, 256), jnp.float32),
        ],
        compiler_params=pltpu.CompilerParams(vmem_limit_bytes=LIMIT),
        name="local_visits",
    )(labels, therm)


def frames_kernel(tile, bias, labels, table, out, term, left, acc):
    chunks, states_k, _ = table.shape
    frames = bias.shape[1]
    groups = states_k // 8

    def pick(step, top_term):
        at = pl.ds(pl.multiple_of(step * LANES, LANES), LANES)
        lab = jnp.broadcast_to(labels[:, at], (8, LANES))
        low = jnp.bitwise_and(lab, LANES - 1)
        high = jnp.right_shift(lab, 7)
        found = [jnp.zeros((8, LANES), jnp.float32)] * groups
        for c in range(chunks):
            here = high == c
            for g in range(groups):
                piece = table[c, g * 8 : (g + 1) * 8, :]
                value = jnp.take_along_axis(piece, low, axis=1)
                found[g] = jnp.where(here, value, found[g])
        cost = [bias[g * 8 : (g + 1) * 8, at] for g in range(groups)]
        scores = [found[g] - cost[g] for g in range(groups)]
        top = jnp.max(functools.reduce(jnp.maximum, scores), axis=0, keepdims=True)
        total = sum(jnp.exp(s - top) for s in scores)
        logl = top + jnp.log(jnp.sum(total, axis=0, keepdims=True))
        made = []
        for g in range(groups):
            value = -cost[g] - logl
            term[g * 8 : (g + 1) * 8, at] = value
            made.append(jnp.maximum(top_term[g], value))
        return tuple(made)

    start = (jnp.full((8, LANES), -jnp.inf, jnp.float32),) * groups
    best = lax.fori_loop(0, frames // LANES, pick, start)
    shift = jnp.concatenate([jnp.max(b, axis=1, keepdims=True) for b in best], axis=0)
    acc[...] = jnp.zeros_like(acc)
    highs = chunks // 2

    @pl.loop(0, frames // tile)
    def _(step):
        at = pl.ds(pl.multiple_of(step * tile, tile), tile)
        lab = labels[:, at]
        high = jnp.right_shift(lab, 8)
        weight = jnp.exp(term[:, at] - shift)
        coarse = weight.astype(jnp.bfloat16).astype(jnp.float32)
        fine = weight - coarse
        for h in range(highs):
            here = high == h
            left[pl.ds(h * states_k, states_k), :] = jnp.where(
                here, coarse, 0.0
            ).astype(jnp.bfloat16)
            left[pl.ds((highs + h) * states_k, states_k), :] = jnp.where(
                here, fine, 0.0
            ).astype(jnp.bfloat16)
        acc[...] += dot_nt(left[...], low_onehot(lab))

    for h in range(highs):
        total = acc[pl.ds(h * states_k, states_k), :] + acc[
            pl.ds((highs + h) * states_k, states_k), :
        ]
        logged = shift + jnp.log(total)
        out[2 * h] = logged[:, :LANES]
        out[2 * h + 1] = logged[:, LANES:]


def frame_sums(bias, labels, table):
    tile = 1024
    chunks, states_k, _ = table.shape
    rows = chunks * states_k
    return pl.pallas_call(
        functools.partial(frames_kernel, tile),
        out_shape=jax.ShapeDtypeStruct(table.shape, jnp.float32),
        in_specs=[VMEM] * 3,
        out_specs=VMEM,
        scratch_shapes=[
            pltpu.VMEM(bias.shape, jnp.float32),
            pltpu.VMEM((rows, tile), jnp.bfloat16),
            pltpu.VMEM((rows, 256), jnp.float32),
        ],
        compiler_params=pltpu.CompilerParams(vmem_limit_bytes=LIMIT),
        name="frame_sums",
    )(bias, labels, table)


class Place:
    def __init__(self, traj, mstate):
        self.traj, self.mstate, self.all = traj, mstate, traj * mstate
        self.t, self.m = lax.axis_index("traj"), lax.axis_index("mstate")
        self.p = self.t * mstate + self.m
        self.chunk = self.m * traj + self.t

    def other(self, o):
        q = lax.rem(self.p + o, self.all)
        t, m = lax.div(q, self.mstate), lax.rem(q, self.mstate)
        return q, t, m, m * self.traj + t

    def greet(self):
        barrier = pltpu.get_barrier_semaphore()

        @pl.loop(1, self.all)
        def _(o):
            _, t, m, _ = self.other(o)
            pl.semaphore_signal(barrier, inc=1, device_id=(t, m), device_id_type=MESH)

        pl.semaphore_wait(barrier, self.all - 1)


def remote(src, dst, send, recv, to):
    return pltpu.make_async_remote_copy(
        src_ref=src, dst_ref=dst, send_sem=send, recv_sem=recv,
        device_id=to, device_id_type=MESH,
    )


class Scatter:
    def __init__(self, place, src, held, send, recv):
        self.args = (place, src, held, send, recv)

    def start(self):
        place, src, held, send, recv = self.args

        @pl.loop(1, place.all)
        def _(o):
            _, t, m, c = place.other(o)
            remote(src.at[c], held.at[place.p], send.at[o], recv.at[o], (t, m)).start()

        held[place.p] = src[place.chunk]

    def wait(self):
        place, src, held, send, recv = self.args

        @pl.loop(1, place.all)
        def _(o):
            q, t, m, c = place.other(place.all - o)
            remote(src.at[c], held.at[q], send.at[o], recv.at[o], (t, m)).wait()


class Rows:
    def __init__(self, place, src, held, send, recv, each):
        self.args = (place, src, held, send, recv, each)

    def start(self):
        place, src, held, send, recv, each = self.args

        @pl.loop(1, place.traj)
        def _(o):
            t = lax.rem(place.t + o, place.traj)
            block = src.at[t] if each else src.at[place.t]
            remote(block, held.at[place.t], send.at[o], recv.at[o], (t, place.m)).start()

        if each:
            held[place.t] = src[place.t]

    def wait(self):
        place, src, held, send, recv, each = self.args

        @pl.loop(1, place.traj)
        def _(o):
            t = lax.rem(place.t + place.traj - o, place.traj)
            remote(src.at[t], held.at[t], send.at[o], recv.at[o], (t, place.m)).wait()


class Gather:
    def __init__(self, place, whole, send, recv):
        self.args = (place, whole, send, recv)

    def start(self):
        place, whole, send, recv = self.args

        @pl.loop(1, place.all)
        def _(o):
            _, t, m, _ = place.other(o)
            own = whole.at[place.chunk]
            remote(own, own, send.at[o], recv.at[o], (t, m)).start()

    def wait(self):
        place, whole, send, recv = self.args

        @pl.loop(1, place.all)
        def _(o):
            _, t, m, c = place.other(place.all - o)
            got = whole.at[c]
            remote(got, got, send.at[o], recv.at[o], (t, m)).wait()


def level_kernel(sizes, first, part, vis, free, level, mult, *rest):
    place = Place(*sizes)
    if first:
        vis_out, held, s0, r0, s1, r1, held_vis, s2, r2 = rest
    else:
        held, s0, r0, s1, r1 = rest
    place.greet()
    rows = Rows(place, part, held, s0, r0, True)
    rows.start()
    if first:
        scatter = Scatter(place, vis, held_vis, s2, r2)
        scatter.start()
    rows.wait()
    inner = 0.5 + sum(held[i] for i in range(place.traj))
    mult[...] = jnp.log(inner)
    if first:
        scatter.wait()
        visits = sum(held_vis[i] for i in range(place.all))
        vis_out[...] = visits
    else:
        visits = vis[...]
    level[place.chunk] = jnp.log(inner + visits) + free[...]
    gather = Gather(place, level, s1, r1)
    gather.start()
    gather.wait()


def levels(sizes, first, part, vis, free):
    traj, mstate = sizes
    every = traj * mstate
    block = part.shape[1:]
    one = jax.ShapeDtypeStruct(block, jnp.float32)
    dma = pltpu.SemaphoreType.DMA
    scratch = [pltpu.VMEM((traj, *block), jnp.float32), dma((traj,)), dma((traj,)), dma((every,)), dma((every,))]
    if first:
        scratch += [pltpu.VMEM((every, *block), jnp.float32), dma((every,)), dma((every,))]
    shapes = [jax.ShapeDtypeStruct((every, *block), jnp.float32), one] + [one] * first
    return pl.pallas_call(
        functools.partial(level_kernel, sizes, first),
        out_shape=shapes,
        in_specs=[VMEM] * 3,
        out_specs=[VMEM] * len(shapes),
        scratch_shapes=scratch,
        compiler_params=pltpu.CompilerParams(
            collective_id=0 if first else 1, has_side_effects=True, vmem_limit_bytes=LIMIT
        ),
        name="levels_first" if first else "levels_later",
    )(part, vis, free)


def free_kernel(sizes, last, logged, mult, out, *rest):
    place = Place(*sizes)
    if last:
        held, s0, r0, s1, r1 = rest
    else:
        free_out, held, s0, r0, s1, r1 = rest
    place.greet()
    scatter = Scatter(place, logged, held, s0, r0)
    scatter.start()
    scatter.wait()
    top = functools.reduce(jnp.maximum, [held[i] for i in range(place.all)])
    top = jnp.maximum(top, -3e38)
    total = sum(jnp.exp(held[i] - top) for i in range(place.all))
    free = -(top + jnp.log(total))
    if last:
        out[place.t, 0] = free
        out[place.t, 1] = mult[...]
        gather = Rows(place, out, out, s1, r1, False)
    else:
        free_out[...] = free
        out[place.chunk] = 0.5 * (mult[...] - free)
        gather = Gather(place, out, s1, r1)
    gather.start()
    gather.wait()


def free_energies(sizes, last, logged, mult):
    traj, mstate = sizes
    every = traj * mstate
    block = mult.shape
    dma = pltpu.SemaphoreType.DMA
    if last:
        shapes = [jax.ShapeDtypeStruct((traj, 2, *block), jnp.float32)]
        second = traj
    else:
        shapes = [jax.ShapeDtypeStruct(s, jnp.float32) for s in ((every, *block), block)]
        second = every
    return pl.pallas_call(
        functools.partial(free_kernel, sizes, last),
        out_shape=shapes,
        in_specs=[VMEM] * 2,
        out_specs=[VMEM] * len(shapes),
        scratch_shapes=[
            pltpu.VMEM((every, *block), jnp.float32),
            dma((every,)), dma((every,)), dma((second,)), dma((second,)),
        ],
        compiler_params=pltpu.CompilerParams(
            collective_id=3 if last else 2, has_side_effects=True, vmem_limit_bytes=LIMIT
        ),
        name="free_last" if last else "free_earlier",
    )(logged, mult)


def chunked(sizes, bias, labels, therm_index, counts, free_start, mult_start):
    states_k, width = free_start.shape
    every = sizes[0] * sizes[1]
    t, m = lax.axis_index("traj"), lax.axis_index("mstate")
    where = jnp.stack([t, m]).astype(jnp.int32)
    lab, therm = labels[None, :], therm_index[None, :]
    half = 0.5 * (mult_start - free_start)
    half = half.reshape(states_k, every, LANES).transpose(1, 0, 2)
    free = lax.dynamic_slice_in_dim(free_start, (m * sizes[0] + t) * LANES, LANES, 1)
    vis = local_visits(lab, therm, states_k, width)
    for step in range(ITERS):
        part = mult_partial(where, counts, half)
        if step == 0:
            table, mult, vis = levels(sizes, True, part, vis, free)
        else:
            table, mult = levels(sizes, False, part, vis, free)
        logged = frame_sums(bias, lab, table)
        if step < ITERS - 1:
            half, free = free_energies(sizes, False, logged, mult)
    (both,) = free_energies(sizes, True, logged, mult)
    both = both.transpose(1, 2, 0, 3).reshape(2, states_k, sizes[0] * LANES)
    return both[0], both[1]


def unchunked(bias, labels, therm_index, counts, free_start, mult_start):
    states_k = bias.shape[0]
    width = free_start.shape[1]
    col_count = counts.shape[1]
    row_count = counts.shape[2]
    col_start = lax.axis_index("traj") * col_count
    row_start = lax.axis_index("mstate") * row_count
    states = jax.nn.one_hot(therm_index, states_k, dtype=jnp.float32)
    visits = lax.psum(
        jax.ops.segment_sum(states, labels, num_segments=width).T, ("traj", "mstate")
    )
    counts_real = counts.astype(jnp.float32)
    free, mult = (free_start, mult_start)
    for step in range(ITERS):
        half = mult - free
        cols = lax.dynamic_slice_in_dim(half, col_start, col_count, 1)
        rows = lax.dynamic_slice_in_dim(half, row_start, row_count, 1)
        weight = jax.nn.sigmoid(rows[:, None, :] - cols[:, :, None])
        row_total = lax.psum(jnp.sum(counts_real * weight, axis=1), "traj")
        mult = lax.all_gather(jnp.log(0.5 + row_total), "mstate", axis=1, tiled=True)
        level = jnp.log(jnp.exp(mult) + visits) + free
        scores = jnp.take(level, labels, axis=1) - bias
        top = jnp.max(scores, axis=0)
        logl = top + jnp.log(jnp.sum(jnp.exp(scores - top[None, :]), axis=0))
        term = -bias - logl[None, :]
        shift = lax.pmax(jnp.max(term, axis=1), ("traj", "mstate"))
        weights = jnp.exp(term - shift[:, None])
        local_total = jax.ops.segment_sum(weights.T, labels, num_segments=width).T
        total = lax.psum(local_total, ("traj", "mstate"))
        free = -(shift[:, None] + jnp.log(total))
    free_out = lax.dynamic_slice_in_dim(free, row_start, row_count, 1)
    mult_out = lax.dynamic_slice_in_dim(mult, row_start, row_count, 1)
    return (free_out, mult_out)


def solution(mesh):
    sizes = (mesh.shape["traj"], mesh.shape["mstate"])

    def per_device(bias, labels, therm_index, counts, free_start, mult_start):
        args = (bias, labels, therm_index, counts, free_start, mult_start)
        fits = (
            free_start.shape[1] == sizes[0] * sizes[1] * LANES
            and counts.shape[1] % LANES == 0
            and bias.shape[1] % 1024 == 0
            and bias.shape[0] % 16 == 0
        )
        return chunked(sizes, *args) if fits else unchunked(*args)

    placed = (
        P(None, ("traj", "mstate")),
        P(("traj", "mstate")),
        P(("traj", "mstate")),
        P(None, "traj", "mstate"),
        P(),
        P(),
    )
    return jax.shard_map(
        per_device,
        mesh=mesh,
        in_specs=placed,
        out_specs=(P(None, "mstate"), P(None, "mstate")),
        check_vma=False,
    )
```

```python
import functools

import jax
import jax.numpy as jnp
from jax import lax
from jax.experimental import pallas as pl
from jax.experimental.pallas import tpu as pltpu
from jax.sharding import PartitionSpec as P

ITERS = 2
LANES = 128
MESH = pl.DeviceIdType.MESH
VMEM = pl.BlockSpec(memory_space=pltpu.VMEM)
LIMIT = 48 * 1024 * 1024


def mult_kernel(where, counts, rows, cols, out, spread):
    k = pl.program_id(0)
    chunks = rows.shape[0]
    for piece in range(cols.shape[0]):
        line = cols[piece, pl.ds(k, 1), :]
        spread[pl.ds(piece * LANES, LANES), :] = jnp.transpose(
            jnp.broadcast_to(line, (LANES, LANES))
        )
    own = [jnp.broadcast_to(rows[c, pl.ds(k, 1), :], (8, LANES)) for c in range(chunks)]

    def body(step, sums):
        at = pl.ds(pl.multiple_of(step * 8, 8), 8)
        other = spread[at, :]
        made = []
        for c in range(chunks):
            number = counts[0, at, c * LANES : (c + 1) * LANES].astype(jnp.float32)
            whole = 1.0 + jnp.exp(jnp.minimum(other - own[c], 87.0))
            near = pl.reciprocal(whole, approx=True)
            made.append(sums[c] + (number * near) * (2.0 - whole * near))
        return tuple(made)

    zero = jnp.zeros((8, LANES), jnp.float32)
    sums = lax.fori_loop(0, counts.shape[1] // 8, body, (zero,) * chunks, unroll=4)
    for c in range(chunks):
        out[c, pl.ds(k, 1), :] = jnp.sum(sums[c], axis=0, keepdims=True)


def mult_partial(where, counts, half):
    states_k, cols, rows = counts.shape
    r, c = rows // LANES, cols // LANES
    return pl.pallas_call(
        mult_kernel,
        grid_spec=pltpu.PrefetchScalarGridSpec(
            num_scalar_prefetch=1,
            grid=(states_k,),
            in_specs=[
                pl.BlockSpec((1, cols, rows), lambda k, w: (k, 0, 0)),
                pl.BlockSpec((r, states_k, LANES), lambda k, w: (w[1], 0, 0)),
                pl.BlockSpec((c, states_k, LANES), lambda k, w: (w[0], 0, 0)),
            ],
            out_specs=pl.BlockSpec((r, states_k, LANES), lambda k, w: (0, 0, 0)),
            scratch_shapes=[pltpu.VMEM((cols, LANES), jnp.float32)],
        ),
        out_shape=jax.ShapeDtypeStruct((r, states_k, LANES), jnp.float32),
        compiler_params=pltpu.CompilerParams(vmem_limit_bytes=LIMIT),
        name="mult_partial",
    )(where, counts, half, half)


def low_onehot(lab):
    low = jnp.bitwise_and(lab, 255)
    lines = lax.broadcasted_iota(jnp.int32, (256, lab.shape[1]), 0)
    return jnp.where(lines == low, 1.0, 0.0).astype(jnp.bfloat16)


def dot_nt(a, b):
    return lax.dot_general(
        a, b, (((1,), (1,)), ((), ())), preferred_element_type=jnp.float32
    )


def visits_kernel(tile, states_k, labels, therm, out, left, acc):
    highs = out.shape[0] // 2
    acc[...] = jnp.zeros_like(acc)

    @pl.loop(0, labels.shape[1] // tile)
    def _(step):
        at = pl.ds(pl.multiple_of(step * tile, tile), tile)
        lab = labels[:, at]
        high = jnp.right_shift(lab, 8)
        lines = lax.broadcasted_iota(jnp.int32, (states_k, tile), 0)
        member = jnp.where(lines == therm[:, at], 1.0, 0.0)
        for h in range(highs):
            left[pl.ds(h * states_k, states_k), :] = jnp.where(
                high == h, member, 0.0
            ).astype(jnp.bfloat16)
        acc[...] += dot_nt(left[...], low_onehot(lab))

    for h in range(highs):
        at = pl.ds(h * states_k, states_k)
        out[2 * h] = acc[at, :LANES]
        out[2 * h + 1] = acc[at, LANES:]


def local_visits(labels, therm, states_k, width):
    tile = 1024
    rows = width // 256 * states_k
    return pl.pallas_call(
        functools.partial(visits_kernel, tile, states_k),
        out_shape=jax.ShapeDtypeStruct((width // LANES, states_k, LANES), jnp.float32),
        in_specs=[VMEM] * 2,
        out_specs=VMEM,
        scratch_shapes=[
            pltpu.VMEM((rows, tile), jnp.bfloat16),
            pltpu.VMEM((rows, 256), jnp.float32),
        ],
        compiler_params=pltpu.CompilerParams(vmem_limit_bytes=LIMIT),
        name="local_visits",
    )(labels, therm)


def frames_kernel(tile, bias, labels, table, out, term, left, acc):
    chunks, states_k, _ = table.shape
    frames = bias.shape[1]
    groups = states_k // 8

    def pick(step, top_term):
        at = pl.ds(pl.multiple_of(step * LANES, LANES), LANES)
        lab = jnp.broadcast_to(labels[:, at], (8, LANES))
        low = jnp.bitwise_and(lab, LANES - 1)
        high = jnp.right_shift(lab, 7)
        found = [jnp.zeros((8, LANES), jnp.float32)] * groups
        for c in range(chunks):
            here = high == c
            for g in range(groups):
                piece = table[c, g * 8 : (g + 1) * 8, :]
                value = jnp.take_along_axis(piece, low, axis=1)
                found[g] = jnp.where(here, value, found[g])
        cost = [bias[g * 8 : (g + 1) * 8, at] for g in range(groups)]
        scores = [found[g] - cost[g] for g in range(groups)]
        top = jnp.max(functools.reduce(jnp.maximum, scores), axis=0, keepdims=True)
        total = sum(jnp.exp(s - top) for s in scores)
        logl = top + jnp.log(jnp.sum(total, axis=0, keepdims=True))
        made = []
        for g in range(groups):
            value = -cost[g] - logl
            term[g * 8 : (g + 1) * 8, at] = value
            made.append(jnp.maximum(top_term[g], value))
        return tuple(made)

    start = (jnp.full((8, LANES), -jnp.inf, jnp.float32),) * groups
    best = lax.fori_loop(0, frames // LANES, pick, start)
    shift = jnp.concatenate([jnp.max(b, axis=1, keepdims=True) for b in best], axis=0)
    acc[...] = jnp.zeros_like(acc)
    highs = chunks // 2

    @pl.loop(0, frames // tile)
    def _(step):
        at = pl.ds(pl.multiple_of(step * tile, tile), tile)
        lab = labels[:, at]
        high = jnp.right_shift(lab, 8)
        weight = jnp.exp(term[:, at] - shift)
        coarse = weight.astype(jnp.bfloat16).astype(jnp.float32)
        fine = weight - coarse
        for h in range(highs):
            here = high == h
            left[pl.ds(h * states_k, states_k), :] = jnp.where(
                here, coarse, 0.0
            ).astype(jnp.bfloat16)
            left[pl.ds((highs + h) * states_k, states_k), :] = jnp.where(
                here, fine, 0.0
            ).astype(jnp.bfloat16)
        acc[...] += dot_nt(left[...], low_onehot(lab))

    for h in range(highs):
        total = acc[pl.ds(h * states_k, states_k), :] + acc[
            pl.ds((highs + h) * states_k, states_k), :
        ]
        logged = shift + jnp.log(total)
        out[2 * h] = logged[:, :LANES]
        out[2 * h + 1] = logged[:, LANES:]


def frame_sums(bias, labels, table):
    tile = 1024
    chunks, states_k, _ = table.shape
    rows = chunks * states_k
    return pl.pallas_call(
        functools.partial(frames_kernel, tile),
        out_shape=jax.ShapeDtypeStruct(table.shape, jnp.float32),
        in_specs=[VMEM] * 3,
        out_specs=VMEM,
        scratch_shapes=[
            pltpu.VMEM(bias.shape, jnp.float32),
            pltpu.VMEM((rows, tile), jnp.bfloat16),
            pltpu.VMEM((rows, 256), jnp.float32),
        ],
        compiler_params=pltpu.CompilerParams(vmem_limit_bytes=LIMIT),
        name="frame_sums",
    )(bias, labels, table)


class Place:
    def __init__(self, traj, mstate):
        self.traj, self.mstate = traj, mstate
        self.rows = 2 if traj % 2 == 0 else 1
        self.planes = traj // self.rows
        self.flat = self.rows * mstate
        self.t, self.m = lax.axis_index("traj"), lax.axis_index("mstate")
        self.z, self.y = lax.div(self.t, self.rows), lax.rem(self.t, self.rows)
        self.g = self.y * mstate + self.m

    def beside(self, o):
        q = lax.rem(self.g + o, self.flat)
        return q, lax.div(q, self.mstate), lax.rem(q, self.mstate)

    def plane(self, o):
        return lax.rem(self.z + o, self.planes)

    def at(self, z, y, m):
        return (z * self.rows + y, m)

    def greet(self):
        barrier = pltpu.get_barrier_semaphore()
        for o in range(1, self.flat):
            _, y, m = self.beside(o)
            pl.semaphore_signal(
                barrier, inc=1, device_id=self.at(self.z, y, m), device_id_type=MESH
            )
        for o in range(1, self.planes):
            for y in range(self.rows):
                pl.semaphore_signal(
                    barrier, inc=1, device_id=self.at(self.plane(o), y, self.m),
                    device_id_type=MESH,
                )
        pl.semaphore_wait(barrier, self.flat - 1 + (self.planes - 1) * self.rows)


def remote(src, dst, send, recv, to):
    return pltpu.make_async_remote_copy(
        src_ref=src, dst_ref=dst, send_sem=send, recv_sem=recv,
        device_id=to, device_id_type=MESH,
    )


def add_all(blocks):
    return sum(blocks)


def add_logs(blocks):
    top = jnp.maximum(functools.reduce(jnp.maximum, blocks), -3e38)
    return top + jnp.log(sum(jnp.exp(b - top) for b in blocks))


class Scatter:
    def __init__(self, place, join, src, near, stage, far, s0, r0, s1, r1):
        self.place, self.join = place, join
        self.src, self.near, self.stage, self.far = src, near, stage, far
        self.s0, self.r0, self.s1, self.r1 = s0, r0, s1, r1

    def start(self):
        p = self.place
        for o in range(1, p.flat):
            _, y, m = p.beside(o)
            remote(
                self.src.at[m, :, y], self.near.at[p.g], self.s0.at[o], self.r0.at[o],
                p.at(p.z, y, m),
            ).start()
        for z in range(p.planes):
            self.near[p.g, z] = self.src[p.m, z, p.y]

    def middle(self):
        p = self.place
        for o in range(1, p.flat):
            q, y, m = p.beside(p.flat - o)
            remote(
                self.src.at[m, :, y], self.near.at[q], self.s0.at[o], self.r0.at[o],
                p.at(p.z, y, m),
            ).wait()
        for z in range(p.planes):
            self.stage[z] = self.join([self.near[i, z] for i in range(p.flat)])
        for o in range(1, p.planes):
            z = p.plane(o)
            remote(
                self.stage.at[z], self.far.at[p.z], self.s1.at[o], self.r1.at[o],
                p.at(z, p.y, p.m),
            ).start()
        self.far[p.z] = self.stage[p.z]

    def finish(self):
        p = self.place
        for o in range(1, p.planes):
            z = p.plane(p.planes - o)
            remote(
                self.stage.at[z], self.far.at[z], self.s1.at[o], self.r1.at[o],
                p.at(z, p.y, p.m),
            ).wait()
        return self.join([self.far[i] for i in range(p.planes)])


def scatter_scratch(sizes, block):
    rows = 2 if sizes[0] % 2 == 0 else 1
    planes, flat = sizes[0] // rows, rows * sizes[1]
    dma = pltpu.SemaphoreType.DMA
    return [
        pltpu.VMEM((flat, planes, *block), jnp.float32),
        pltpu.VMEM((planes, *block), jnp.float32),
        pltpu.VMEM((planes, *block), jnp.float32),
        dma((flat,)), dma((flat,)), dma((planes,)), dma((planes,)),
    ]


def gather_scratch(sizes):
    return scatter_scratch(sizes, (8, LANES))[3:]


def split_shape(sizes, block):
    rows = 2 if sizes[0] % 2 == 0 else 1
    return (sizes[1], sizes[0] // rows, rows, *block)


class Rows:
    def __init__(self, place, src, held, send, recv, each):
        self.args = (place, src, held, send, recv, each)

    def start(self):
        place, src, held, send, recv, each = self.args

        @pl.loop(1, place.traj)
        def _(o):
            t = lax.rem(place.t + o, place.traj)
            block = src.at[t] if each else src.at[place.t]
            remote(block, held.at[place.t], send.at[o], recv.at[o], (t, place.m)).start()

        if each:
            held[place.t] = src[place.t]

    def wait(self):
        place, src, held, send, recv, each = self.args

        @pl.loop(1, place.traj)
        def _(o):
            t = lax.rem(place.t + place.traj - o, place.traj)
            remote(src.at[t], held.at[t], send.at[o], recv.at[o], (t, place.m)).wait()


def gather_all(p, whole, s0, r0, s1, r1):
    own = whole.at[p.m, p.z, p.y]
    for o in range(1, p.planes):
        remote(own, own, s1.at[o], r1.at[o], p.at(p.plane(o), p.y, p.m)).start()
    for o in range(1, p.planes):
        z = p.plane(p.planes - o)
        got = whole.at[p.m, z, p.y]
        remote(got, got, s1.at[o], r1.at[o], p.at(z, p.y, p.m)).wait()
    column = whole.at[p.m, :, p.y]
    for o in range(1, p.flat):
        _, y, m = p.beside(o)
        remote(column, column, s0.at[o], r0.at[o], p.at(p.z, y, m)).start()
    for o in range(1, p.flat):
        _, y, m = p.beside(p.flat - o)
        got = whole.at[m, :, y]
        remote(got, got, s0.at[o], r0.at[o], p.at(p.z, y, m)).wait()


def level_kernel(sizes, first, part, vis, free, level, mult, *rest):
    place = Place(*sizes)
    if first:
        vis_out, held, s, r, *rest = rest
    else:
        held, s, r, *rest = rest
    place.greet()
    rows = Rows(place, part, held, s, r, True)
    rows.start()
    if first:
        scatter = Scatter(place, add_all, vis, *rest[4:])
        scatter.start()
        scatter.middle()
    rows.wait()
    inner = 0.5 + sum(held[i] for i in range(place.traj))
    mult[...] = jnp.log(inner)
    if first:
        visits = scatter.finish()
        vis_out[...] = visits
    else:
        visits = vis[...]
    level[place.m, place.z, place.y] = jnp.log(inner + visits) + free[...]
    gather_all(place, level, *rest[:4])


def levels(sizes, first, part, vis, free):
    traj = sizes[0]
    block = part.shape[1:]
    one = jax.ShapeDtypeStruct(block, jnp.float32)
    dma = pltpu.SemaphoreType.DMA
    scratch = [pltpu.VMEM((traj, *block), jnp.float32), dma((traj,)), dma((traj,))]
    scratch += gather_scratch(sizes)
    if first:
        scratch += scatter_scratch(sizes, block)
        vis = vis.reshape(split_shape(sizes, block))
    whole = jax.ShapeDtypeStruct(split_shape(sizes, block), jnp.float32)
    shapes = [whole, one] + [one] * first
    table, *others = pl.pallas_call(
        functools.partial(level_kernel, sizes, first),
        out_shape=shapes,
        in_specs=[VMEM] * 3,
        out_specs=[VMEM] * len(shapes),
        scratch_shapes=scratch,
        compiler_params=pltpu.CompilerParams(
            collective_id=0 if first else 1, has_side_effects=True, vmem_limit_bytes=LIMIT
        ),
        name="levels_first" if first else "levels_later",
    )(part, vis, free)
    return table.reshape(-1, *block), *others


def free_kernel(sizes, last, logged, mult, out, *rest):
    place = Place(*sizes)
    if not last:
        free_out, *rest = rest
    place.greet()
    scatter = Scatter(place, add_logs, logged, *rest[:7])
    scatter.start()
    scatter.middle()
    free = -scatter.finish()
    if last:
        out[place.t, 0] = free
        out[place.t, 1] = mult[...]
        rows = Rows(place, out, out, *rest[7:], False)
        rows.start()
        rows.wait()
    else:
        free_out[...] = free
        out[place.m, place.z, place.y] = mult[...] - free
        gather_all(place, out, *rest[7:])


def free_energies(sizes, last, logged, mult):
    traj = sizes[0]
    block = mult.shape
    split = split_shape(sizes, block)
    dma = pltpu.SemaphoreType.DMA
    scratch = scatter_scratch(sizes, block)
    if last:
        shapes = [jax.ShapeDtypeStruct((traj, 2, *block), jnp.float32)]
        scratch += [dma((traj,)), dma((traj,))]
    else:
        shapes = [jax.ShapeDtypeStruct(a, jnp.float32) for a in (split, block)]
        scratch += gather_scratch(sizes)
    made = pl.pallas_call(
        functools.partial(free_kernel, sizes, last),
        out_shape=shapes,
        in_specs=[VMEM] * 2,
        out_specs=[VMEM] * len(shapes),
        scratch_shapes=scratch,
        compiler_params=pltpu.CompilerParams(
            collective_id=3 if last else 2, has_side_effects=True, vmem_limit_bytes=LIMIT
        ),
        name="free_last" if last else "free_earlier",
    )(logged.reshape(split), mult)
    return made if last else (made[0].reshape(-1, *block), made[1])


def chunked(sizes, bias, labels, therm_index, counts, free_start, mult_start):
    states_k, width = free_start.shape
    every = sizes[0] * sizes[1]
    t, m = lax.axis_index("traj"), lax.axis_index("mstate")
    where = jnp.stack([t, m]).astype(jnp.int32)
    lab, therm = labels[None, :], therm_index[None, :]
    half = mult_start - free_start
    half = half.reshape(states_k, every, LANES).transpose(1, 0, 2)
    free = lax.dynamic_slice_in_dim(free_start, (m * sizes[0] + t) * LANES, LANES, 1)
    vis = local_visits(lab, therm, states_k, width)
    for step in range(ITERS):
        part = mult_partial(where, counts, half)
        if step == 0:
            table, mult, vis = levels(sizes, True, part, vis, free)
        else:
            table, mult = levels(sizes, False, part, vis, free)
        logged = frame_sums(bias, lab, table)
        if step < ITERS - 1:
            half, free = free_energies(sizes, False, logged, mult)
    (both,) = free_energies(sizes, True, logged, mult)
    both = both.transpose(1, 2, 0, 3).reshape(2, states_k, sizes[0] * LANES)
    return both[0], both[1]


def unchunked(bias, labels, therm_index, counts, free_start, mult_start):
    states_k = bias.shape[0]
    width = free_start.shape[1]
    col_count = counts.shape[1]
    row_count = counts.shape[2]
    col_start = lax.axis_index("traj") * col_count
    row_start = lax.axis_index("mstate") * row_count
    states = jax.nn.one_hot(therm_index, states_k, dtype=jnp.float32)
    visits = lax.psum(
        jax.ops.segment_sum(states, labels, num_segments=width).T, ("traj", "mstate")
    )
    counts_real = counts.astype(jnp.float32)
    free, mult = (free_start, mult_start)
    for step in range(ITERS):
        half = mult - free
        cols = lax.dynamic_slice_in_dim(half, col_start, col_count, 1)
        rows = lax.dynamic_slice_in_dim(half, row_start, row_count, 1)
        weight = jax.nn.sigmoid(rows[:, None, :] - cols[:, :, None])
        row_total = lax.psum(jnp.sum(counts_real * weight, axis=1), "traj")
        mult = lax.all_gather(jnp.log(0.5 + row_total), "mstate", axis=1, tiled=True)
        level = jnp.log(jnp.exp(mult) + visits) + free
        scores = jnp.take(level, labels, axis=1) - bias
        top = jnp.max(scores, axis=0)
        logl = top + jnp.log(jnp.sum(jnp.exp(scores - top[None, :]), axis=0))
        term = -bias - logl[None, :]
        shift = lax.pmax(jnp.max(term, axis=1), ("traj", "mstate"))
        weights = jnp.exp(term - shift[:, None])
        local_total = jax.ops.segment_sum(weights.T, labels, num_segments=width).T
        total = lax.psum(local_total, ("traj", "mstate"))
        free = -(shift[:, None] + jnp.log(total))
    free_out = lax.dynamic_slice_in_dim(free, row_start, row_count, 1)
    mult_out = lax.dynamic_slice_in_dim(mult, row_start, row_count, 1)
    return (free_out, mult_out)


def solution(mesh):
    sizes = (mesh.shape["traj"], mesh.shape["mstate"])

    def per_device(bias, labels, therm_index, counts, free_start, mult_start):
        args = (bias, labels, therm_index, counts, free_start, mult_start)
        fits = (
            free_start.shape[1] == sizes[0] * sizes[1] * LANES
            and counts.shape[1] % LANES == 0
            and bias.shape[1] % 1024 == 0
            and bias.shape[0] % 16 == 0
        )
        return chunked(sizes, *args) if fits else unchunked(*args)

    placed = (
        P(None, ("traj", "mstate")),
        P(("traj", "mstate")),
        P(("traj", "mstate")),
        P(None, "traj", "mstate"),
        P(),
        P(),
    )
    return jax.shard_map(
        per_device,
        mesh=mesh,
        in_specs=placed,
        out_specs=(P(None, "mstate"), P(None, "mstate")),
        check_vma=False,
    )
```
